128 devices in a mesh: grp: 2 (over y_hi), rows: 64 (over y_lo, z, x, core).
Axes of the slice: x: 4, y: 4 (y_hi: 2, y_lo: 2; y = y_hi * 2 + y_lo), z: 4, core: 2. Of those that a mesh axis runs over, the one named last changes fastest.
Arguments:
- bvals: bfloat16 [2, 98304, 6144], P('grp', 'rows'), may hold values from -16 to 16
- gap: float32 [2, 98304], P('grp', 'rows'), may hold values from 0.2 to 2
- live: int32 [2, 64], P('grp', 'rows'), may hold values from 192 to 1536, as said below
- laplace: int32 [1], replicated, may hold values from 0 to 5
Outputs:
- panels: bfloat16 [2, 98304, 512], P('grp', 'rows')
The draws below stay inside these ranges and needn't reach their ends.
Inputs may be any that keep to these rules, and one draw needn't show every extreme that they name: Each device's live rows are its first ones; live[0, d] lies between 1152 and 1536, live[1, d] between 192 and 512.
All inputs are finite; a program needn't handle non-finite values.
Results may differ from the reference program's by a relative error of at most 0.0057.
Values may be sent and summed in bfloat16 or wider, within the bound.
No kernel may reach another device: no remote copies, remote signals or barrier semaphores. Data moves between devices by JAX's collectives and lax.ppermute only.
A program may use at most 192 MiB of HBM per device.

```python
import math
import jax
import jax.numpy as jnp
from jax import lax

AUX = 6144
PANEL = 512
ROW_DEV = 1536
ROWS = 98304


def draw_live(key, part):
    key = jax.random.fold_in(key, 7)
    keys = jax.random.split(key, 4)
    owners = ROWS // ROW_DEV
    first = jax.random.randint(keys[0], (owners,), 3 * ROW_DEV // 4, ROW_DEV + 1)
    second = jax.random.randint(keys[1], (owners,), ROW_DEV // 8, ROW_DEV // 3 + 1)
    full_owner = jax.random.randint(keys[2], (), 0, owners)
    least_owner = jax.random.randint(keys[3], (), 0, owners)
    position = jnp.arange(owners)
    first = jnp.where(position == full_owner, ROW_DEV, first)
    second = jnp.where(position == least_owner, ROW_DEV // 8, second)
    return jnp.stack([first, second]).astype(jnp.int32)


def strengthened(drawn, own_key, source, target, shards_of, factor):
    def block_of(dim):
        return (jnp.arange(drawn.shape[dim]) // (drawn.shape[dim] // shards_of)).reshape((-1,) + (1,) * (drawn.ndim - 1 - dim))

    near = jax.random.permutation(own_key, shards_of)[block_of(target)]
    other_side = (block_of(target) + shards_of // 2) % shards_of
    return jnp.where((block_of(source) == near) | (block_of(source) == other_side), factor * drawn, drawn)


def block_levels(key, shape, cuts, smallest, high):
    loudness = 1.0
    for dim, shards_of in cuts:
        heights = jax.random.uniform(jax.random.fold_in(jax.random.fold_in(key, 6), dim), (shards_of,), jnp.float32, smallest / len(cuts), high / len(cuts))
        loudness = loudness * jnp.repeat(jnp.exp(heights), shape[dim] // shards_of).reshape((-1,) + (1,) * (len(shape) - 1 - dim))
    return loudness


def heavy_noise(key, shape, deviation, reach, cuts, heavy, kind=jnp.bfloat16):
    drawn = deviation * jax.random.normal(key, shape, jnp.float32)
    if cuts:
        drawn = drawn * block_levels(key, shape, cuts, -0.22, 0.18)
    return jnp.clip(strengthened(drawn, jax.random.fold_in(key, 3), *heavy), -reach, reach).astype(kind)


def setup_inputs(seed: int = 0) -> dict:
    key_list = jax.random.split(jax.random.key(seed), 5)
    bvals = heavy_noise(key_list[0], (2, ROWS, AUX), 1.0, 16.0, ((0, 2), (1, 64)), (1, 2, 64, 4.0))
    gap = jnp.clip(jnp.exp(math.log(2.0) - 2.3025851 * jax.random.uniform(key_list[1], (2, ROWS), jnp.float32) ** block_levels(key_list[1], (2, ROWS), ((0, 2), (1, 64)), -0.2, 0.2)), 0.2, 2.0)
    live = draw_live(jax.random.fold_in(key_list[4], 71), 0)
    laplace = jax.random.randint(key_list[3], (1,), 0, 6).astype(jnp.int32)
    return dict(bvals=bvals, gap=gap, live=live, laplace=laplace)


def laplace_time(laplace):
    return 0.15 * jnp.exp(laplace[0].astype(jnp.float32) * jnp.log(jnp.float32(1.5)))


def scaled_block(bvals, gap, live, monomer, owner, moment):
    anchor = (owner * ROW_DEV).astype(jnp.int32)
    block_vals = lax.dynamic_slice_in_dim(bvals[monomer], anchor, ROW_DEV, 0)
    rates = lax.dynamic_slice_in_dim(gap[monomer], anchor, ROW_DEV, 0)
    amount = live[monomer][owner]
    position = jnp.arange(ROW_DEV, dtype=jnp.int32)
    factor = jnp.where(position < amount, jnp.exp(-(rates * moment) * 0.5), 0.0)
    return (block_vals * factor[:, None]).astype(jnp.bfloat16)


def gram_panel(bvals, gap, live, monomer, moment):
    owners = jnp.arange(ROWS // ROW_DEV, dtype=jnp.int32)

    def add_owner(total, owner):
        scaled = scaled_block(bvals, gap, live, monomer, owner, moment)
        return total + jnp.dot(scaled.T, scaled[:, :PANEL], preferred_element_type=jnp.float32), None

    total, unused = lax.scan(add_owner, jnp.zeros((AUX, PANEL), jnp.float32), owners)
    return (total / ROWS).astype(jnp.bfloat16)


def panel_rows(bvals, gap, live, monomer, moment, other):
    owners = jnp.arange(ROWS // ROW_DEV, dtype=jnp.int32)

    def one_owner(owner):
        scaled = scaled_block(bvals, gap, live, monomer, owner, moment)
        return jnp.dot(scaled, other, preferred_element_type=jnp.float32).astype(jnp.bfloat16)

    return lax.map(one_owner, owners).reshape(ROWS, PANEL)


def reference(bvals, gap, live, laplace):
    moment = laplace_time(laplace)
    gram_first = gram_panel(bvals, gap, live, 0, moment)
    gram_second = gram_panel(bvals, gap, live, 1, moment)
    panel_first = panel_rows(bvals, gap, live, 0, moment, gram_second)
    panel_second = panel_rows(bvals, gap, live, 1, moment, gram_first)
    return jnp.stack([panel_first, panel_second])
```

```python
import jax
import jax.numpy as jnp
import numpy as np
from jax import lax
from jax.experimental import pallas as pl
from jax.experimental.pallas import tpu as pltpu
from jax.sharding import PartitionSpec as P

PANEL = 512
LANES = 128
SPOTS = 4
GROUP = 384
F32 = jnp.float32
BF16 = jnp.bfloat16
SIDES = (2, 2, SPOTS, SPOTS, 2)
AXES = ("grp", "rows")


def shifted(array, **steps):
    names = ("grp", "y", "z", "x", "core")
    pairs = []
    for source in range(int(np.prod(SIDES))):
        spot = np.unravel_index(source, SIDES)
        goal = [(a + steps.get(n, 0)) % s for a, n, s in zip(spot, names, SIDES)]
        pairs.append((source, int(np.ravel_multi_index(goal, SIDES))))
    return lax.ppermute(array, AXES, pairs)


def scale_into(target, source, factor, width):
    for k in range(width // LANES):
        cut = slice(k * LANES, (k + 1) * LANES)
        target[:, cut] = (source[:, cut].astype(F32) * factor[...]).astype(BF16)


def gram_body(groups_ref, core_ref, b_ref, mine_ref, theirs_ref, f_ref, ma, mb, ta, tb, panel, block):
    @pl.when(pl.program_id(0) == 0)
    def _():
        scale_into(panel.at[:, :256], mine_ref, f_ref, 256)
        scale_into(panel.at[:, 256:], theirs_ref, f_ref, 256)

    scale_into(block, b_ref, f_ref, GROUP)
    product = lax.dot_general(block[...], panel[...], (((0,), (0,)), ((), ())), preferred_element_type=F32)
    for k, out in enumerate((ma, mb, ta, tb)):
        out[0, 0] = product[:, k * LANES : (k + 1) * LANES].astype(BF16)


def gram_parts(groups, core, bvals, factor):
    rows, aux = bvals.shape
    shape = jax.ShapeDtypeStruct((SPOTS, SPOTS, GROUP, LANES), BF16)
    first = pl.BlockSpec((1, 1, GROUP, LANES), lambda s, g, c: (s // SPOTS, s % SPOTS, 0, 0))
    second = pl.BlockSpec((1, 1, GROUP, LANES), lambda s, g, c: (s % SPOTS, s // SPOTS, 0, 0))
    return pl.pallas_call(
        gram_body,
        grid_spec=pltpu.PrefetchScalarGridSpec(
            num_scalar_prefetch=2,
            grid=(SPOTS * SPOTS,),
            in_specs=[
                pl.BlockSpec((rows, GROUP), lambda s, g, c: (0, g[s])),
                pl.BlockSpec((rows, 256), lambda s, g, c: (0, c[0])),
                pl.BlockSpec((rows, 256), lambda s, g, c: (0, 1 - c[0])),
                pl.BlockSpec((rows, LANES), lambda s, g, c: (0, 0)),
            ],
            out_specs=[first, second, first, second],
            scratch_shapes=[pltpu.VMEM((rows, PANEL), BF16), pltpu.VMEM((rows, GROUP), BF16)],
        ),
        out_shape=[shape] * 4,
        compiler_params=pltpu.CompilerParams(vmem_limit_bytes=32 << 20),
        cost_estimate=pl.CostEstimate(flops=2 * rows * aux * PANEL, bytes_accessed=2 * rows * aux, transcendentals=0),
    )(groups, core, bvals, bvals, bvals, factor)


def panel_body(groups_ref, core_ref, b_ref, f_ref, *refs):
    parts, (out_ref, gram, block) = refs[:16], refs[16:]

    @pl.when(pl.program_id(0) == 0)
    def _():
        core = core_ref[0]
        for owner in range(2):
            start = pl.multiple_of(jnp.where(core == owner, 0, 256), 256)
            place = jnp.where(owner == 0, core, 1 - core)
            for i in range(SPOTS):
                for j in range(SPOTS):
                    row = pl.multiple_of(groups_ref[i * SPOTS + j] * GROUP, GROUP)
                    column = pl.multiple_of(place * 256, 256)
                    gram[pl.ds(row, GROUP), pl.ds(column, LANES)] = parts[owner * 8 + i][j]
                    gram[pl.ds(row, GROUP), pl.ds(column + LANES, LANES)] = parts[owner * 8 + 4 + j][i]

    scale_into(block, b_ref, f_ref, block.shape[1])
    out_ref[...] = jnp.dot(block[...], gram[...], preferred_element_type=F32).astype(BF16)


def panel_rows(groups, core, bvals, factor, parts):
    rows, aux = bvals.shape
    step = 256
    whole = pl.BlockSpec((SPOTS, GROUP, LANES), lambda s, g, c: (0, 0, 0))
    return pl.pallas_call(
        panel_body,
        grid_spec=pltpu.PrefetchScalarGridSpec(
            num_scalar_prefetch=2,
            grid=(rows // step,),
            in_specs=[
                pl.BlockSpec((step, aux), lambda s, g, c: (s, 0)),
                pl.BlockSpec((step, LANES), lambda s, g, c: (s, 0)),
            ]
            + [whole] * 16,
            out_specs=pl.BlockSpec((step, PANEL), lambda s, g, c: (s, 0)),
            scratch_shapes=[pltpu.VMEM((aux, PANEL), BF16), pltpu.VMEM((step, aux), BF16)],
        ),
        out_shape=jax.ShapeDtypeStruct((rows, PANEL), BF16),
        compiler_params=pltpu.CompilerParams(vmem_limit_bytes=48 << 20),
        cost_estimate=pl.CostEstimate(flops=2 * rows * aux * PANEL, bytes_accessed=2 * rows * aux, transcendentals=0),
    )(groups, core, bvals, factor, *parts)


def reduced(mine, theirs, first, second):
    got = shifted(theirs, core=1)
    pair = [mine[k].astype(F32) + got[k].astype(F32) for k in range(SPOTS)]
    held = pair[0]
    for arrived in [shifted(pair[k].astype(BF16), **{first: k}) for k in range(1, SPOTS)]:
        held = held + arrived.astype(F32)
    owned = held[0]
    for arrived in [shifted(held[k].astype(BF16), **{second: k}) for k in range(1, SPOTS)]:
        owned = owned + arrived.astype(F32)
    return owned.astype(BF16)


def gathered(owned, first, second):
    row = [owned] + [shifted(owned, **{first: SPOTS - k}) for k in range(1, SPOTS)]
    row = jnp.stack(row)
    plane = [row] + [shifted(row, **{second: SPOTS - k}) for k in range(1, SPOTS)]
    return plane, [shifted(part, core=1) for part in plane]


def on_device(bvals, gap, live, laplace):
    rows_here = bvals.shape[1]
    total_rows = rows_here * lax.axis_size("rows")
    moment = 0.15 * jnp.exp(laplace[0].astype(F32) * jnp.log(F32(1.5)))
    position = jnp.arange(rows_here, dtype=jnp.int32)
    factor = jnp.where(position < live[0, 0], jnp.exp(-(gap[0] * moment) * 0.5), 0.0)
    factor = jnp.broadcast_to(factor[:, None], (rows_here, LANES))
    here = lax.axis_index("rows")
    core, x, z = here % 2, here // 2 % SPOTS, here // 8 % SPOTS
    steps = jnp.arange(SPOTS, dtype=jnp.int32)
    groups = ((x + steps[:, None]) % SPOTS * SPOTS + (z + steps[None, :]) % SPOTS).reshape(-1)
    core = core.reshape(1)

    mine_a, mine_b, theirs_a, theirs_b = gram_parts(groups, core, bvals[0], factor)
    share = jnp.stack([reduced(mine_a, theirs_a, "x", "z"), reduced(mine_b, theirs_b, "z", "x")])
    near, far = shifted(share, grp=1, y=1), shifted(share, grp=1)
    whole = ((near.astype(F32) + far.astype(F32)) / total_rows).astype(BF16)
    own_a, other_a = gathered(whole[0], "z", "x")
    own_b, other_b = gathered(whole[1], "x", "z")
    return panel_rows(groups, core, bvals[0], factor, own_a + own_b + other_a + other_b)[None]


def solution(mesh):
    in_specs = (P("grp", "rows", None), P("grp", "rows"), P("grp", "rows"), P())
    out_specs = P("grp", "rows", None)
    return jax.shard_map(
        on_device, mesh=mesh, in_specs=in_specs, out_specs=out_specs, check_vma=False
    )
```

```python
import jax
import jax.numpy as jnp
import numpy as np
from jax import lax
from jax.experimental import pallas as pl
from jax.experimental.pallas import tpu as pltpu
from jax.sharding import PartitionSpec as P

PANEL = 512
HALF = 256
LANES = 128
SPOTS = 4
GROUP = 384
F32 = jnp.float32
BF16 = jnp.bfloat16
SIDES = (2, 2, SPOTS, SPOTS, 2)
NAMES = ("grp", "y", "z", "x", "core")


def shifted(array, steps):
    pairs = []
    for source in range(int(np.prod(SIDES))):
        spot = np.unravel_index(source, SIDES)
        step = steps[spot[-1]]
        goal = [(a + step.get(n, 0)) % s for a, n, s in zip(spot, NAMES, SIDES)]
        pairs.append((source, int(np.ravel_multi_index(goal, SIDES))))
    return lax.ppermute(array, ("grp", "rows"), pairs)


def along_first(array, step):
    return shifted(array, ({"x": step}, {"z": step}))


def along_second(array, step):
    return shifted(array, ({"z": step}, {"x": step}))


def to_pair(array):
    return shifted(array, ({"core": 1}, {"core": 1}))


def across(array, step):
    return shifted(array, ({"grp": 1, "y": step},) * 2)


WHOLE = pl.BlockSpec(memory_space=pltpu.VMEM)
TABLE = pl.BlockSpec(memory_space=pltpu.SMEM)
FAR = pl.BlockSpec(memory_space=pltpu.HBM)
LARGE = pltpu.CompilerParams(vmem_limit_bytes=48 << 20)


def place_of(here):
    return here % 2, here // 2 % SPOTS, here // 8 % SPOTS


def group_of(core, x, z, k, m):
    by_x = jnp.where(core == 0, k, m)
    by_z = jnp.where(core == 0, m, k)
    return (x + by_x) % SPOTS * SPOTS + (z + by_z) % SPOTS


def gram_body(here_ref, live_ref, laplace_ref, gap_ref, b_ref, *refs):
    theirs, mine = refs[:SPOTS], refs[SPOTS : 2 * SPOTS]
    f_ref, panel, wide, buffers, sems, wide_sem = refs[2 * SPOTS :]
    core, x, z = place_of(here_ref[0])

    def copies(k, h):
        for i in range(2):
            column = pl.multiple_of(group_of(core, x, z, k, 2 * h + i) * GROUP, LANES)
            source = b_ref.at[:, pl.ds(column, GROUP)]
            yield pltpu.make_async_copy(source, buffers.at[h, :, pl.ds(i * GROUP, GROUP)], sems.at[h, i])

    first = pltpu.make_async_copy(b_ref.at[:, :PANEL], wide, wide_sem)
    first.start()
    for h in range(2):
        for copy in copies(0, h):
            copy.start()

    gap = gap_ref[...]
    moment = 0.15 * jnp.exp(jnp.full(gap.shape, laplace_ref[0], jnp.int32).astype(F32) * np.log(np.float32(1.5)))
    position = lax.broadcasted_iota(jnp.int32, gap.shape, 1)
    factor = jnp.where(position < live_ref[0, 0], jnp.exp(-(gap * moment) * 0.5), 0.0)
    f_ref[...] = jnp.broadcast_to(factor, (LANES, gap.shape[1])).T

    first.wait()
    for half, owner in enumerate((1 - core, core)):
        for c in range(0, HALF, LANES):
            piece = wide[:, pl.ds(pl.multiple_of(owner * HALF + c, LANES), LANES)].astype(F32)
            square = f_ref[...] * f_ref[...]
            panel[:, half * HALF + c : half * HALF + c + LANES] = (piece * square).astype(BF16)

    def some(k, unused):
        for h in range(2):
            for copy in copies(k, h):
                copy.wait()
            product = lax.dot_general(
                buffers[h], panel[...], (((0,), (0,)), ((), ())), preferred_element_type=F32
            ).astype(BF16)
            for i in range(2):
                rows = slice(i * GROUP, (i + 1) * GROUP)
                theirs[2 * h + i][k] = product[rows, :HALF]
                for step in range(SPOTS):

                    @pl.when(k == step)
                    def _():
                        mine[step][2 * h + i] = product[rows, HALF:]

            @pl.when(k + 1 < SPOTS)
            def _():
                for copy in copies(k + 1, h):
                    copy.start()

        return unused

    lax.fori_loop(0, SPOTS, some, 0)


def gram_parts(here, live, laplace, gap, bvals):
    rows = bvals.shape[0]
    part = jax.ShapeDtypeStruct((SPOTS, GROUP, HALF), BF16)
    return pl.pallas_call(
        gram_body,
        in_specs=[TABLE, TABLE, TABLE, WHOLE, FAR],
        out_specs=[WHOLE] * (2 * SPOTS + 1),
        out_shape=[part] * (2 * SPOTS) + [jax.ShapeDtypeStruct((rows, LANES), F32)],
        scratch_shapes=[
            pltpu.VMEM((rows, PANEL), BF16),
            pltpu.VMEM((rows, PANEL), BF16),
            pltpu.VMEM((2, rows, 2 * GROUP), BF16),
            pltpu.SemaphoreType.DMA((2, 2)),
            pltpu.SemaphoreType.DMA,
        ],
        compiler_params=LARGE,
    )(here, live, laplace, gap, bvals)


def panel_body(here_ref, b_ref, f_ref, *refs):
    parts, (out_ref, gram) = refs[:-2], refs[-2:]

    @pl.when(pl.program_id(0) == 0)
    def _():
        core, x, z = place_of(here_ref[0])
        for whose, owner in enumerate((1 - core, core)):
            for k in range(SPOTS):
                for m in range(SPOTS):
                    row = pl.multiple_of(group_of(owner, x, z, k, m) * GROUP, GROUP)
                    column = pl.multiple_of(owner * HALF, HALF)
                    gram[pl.ds(row, GROUP), pl.ds(column, HALF)] = parts[whose * SPOTS + k][m]

    total = jnp.dot(b_ref[...], gram[...], preferred_element_type=F32)
    for c in range(0, PANEL, LANES):
        out_ref[:, c : c + LANES] = (total[:, c : c + LANES] * f_ref[...]).astype(BF16)


def panel_rows(here, bvals, factor, parts):
    rows, aux = bvals.shape
    step = 256
    return pl.pallas_call(
        panel_body,
        grid=(rows // step,),
        in_specs=[
            TABLE,
            pl.BlockSpec((step, aux), lambda s: (s, 0)),
            pl.BlockSpec((step, LANES), lambda s: (s, 0)),
        ]
        + [WHOLE] * len(parts),
        out_specs=pl.BlockSpec((step, PANEL), lambda s: (s, 0)),
        out_shape=jax.ShapeDtypeStruct((rows, PANEL), BF16),
        scratch_shapes=[pltpu.VMEM((aux, PANEL), BF16)],
        compiler_params=LARGE,
    )(here, bvals, factor, *parts)


def total_of(arrays):
    total = arrays[0].astype(F32)
    for array in arrays[1:]:
        total = total + array.astype(F32)
    return total


def on_device(bvals, gap, live, laplace):
    bvals = bvals[0]
    total_rows = bvals.shape[0] * lax.axis_size("rows")
    here = lax.axis_index("rows").reshape(1)
    parts = gram_parts(here, live, laplace, gap, bvals)
    theirs, mine, factor = parts[:SPOTS], parts[SPOTS : 2 * SPOTS], parts[-1]

    pairs = {k: total_of([mine[k], to_pair(theirs[k])]) for k in (2, 1, 3, 0)}
    held = total_of([pairs[0]] + [along_first(pairs[k].astype(BF16), k) for k in (2, 1, 3)])
    share = total_of([held[0]] + [along_second(held[k].astype(BF16), k) for k in (2, 1, 3)]).astype(BF16)
    whole = (total_of([across(share, 0), across(share, 1)]) / total_rows).astype(BF16)
    row = jnp.stack([whole] + [along_second(whole, SPOTS - k) for k in range(1, SPOTS)])
    own = [row] + [along_first(row, SPOTS - k) for k in range(1, SPOTS)]
    return panel_rows(here, bvals, factor, [to_pair(part) for part in own] + own)[None]


def solution(mesh):
    in_specs = (P("grp", "rows", None), P("grp", "rows"), P("grp", "rows"), P())
    out_specs = P("grp", "rows", None)
    return jax.shard_map(
        on_device, mesh=mesh, in_specs=in_specs, out_specs=out_specs, check_vma=False
    )
```

```python
import jax
import jax.numpy as jnp
import numpy as np
from jax import lax
from jax.experimental import pallas as pl
from jax.experimental.pallas import tpu as pltpu
from jax.sharding import PartitionSpec as P

PANEL = 512
HALF = 256
LANES = 128
SPOTS = 4
GROUP = 384
F32 = jnp.float32
BF16 = jnp.bfloat16
SIDES = (2, 2, SPOTS, SPOTS, 2)
NAMES = ("grp", "y", "z", "x", "core")


def shifted(array, steps):
    pairs = []
    for source in range(int(np.prod(SIDES))):
        spot = np.unravel_index(source, SIDES)
        step = steps[spot[-1]]
        goal = [(a + step.get(n, 0)) % s for a, n, s in zip(spot, NAMES, SIDES)]
        pairs.append((source, int(np.ravel_multi_index(goal, SIDES))))
    return lax.ppermute(array, ("grp", "rows"), pairs)


def along_first(array, step):
    return shifted(array, ({"x": step}, {"z": step}))


def along_second(array, step):
    return shifted(array, ({"z": step}, {"x": step}))


def to_pair(array):
    return shifted(array, ({"core": 1}, {"core": 1}))


def across(array, step):
    return shifted(array, ({"grp": 1, "y": step},) * 2)


WHOLE = pl.BlockSpec(memory_space=pltpu.VMEM)
TABLE = pl.BlockSpec(memory_space=pltpu.SMEM)
FAR = pl.BlockSpec(memory_space=pltpu.HBM)
LARGE = pltpu.CompilerParams(vmem_limit_bytes=48 << 20)


def place_of(here):
    return here % 2, here // 2 % SPOTS, here // 8 % SPOTS


def group_of(core, x, z, k, m):
    by_x = jnp.where(core == 0, k, m)
    by_z = jnp.where(core == 0, m, k)
    return (x + by_x) % SPOTS * SPOTS + (z + by_z) % SPOTS


SPANS = ((0, 1), (1, 2), (2, 4), (4, 8), (8, 12), (12, 16))
AHEAD = 3


def gram_body(here_ref, live_ref, laplace_ref, gap_ref, b_ref, *refs):
    theirs, mine = refs[:SPOTS], refs[SPOTS : 2 * SPOTS]
    f_ref, panel, wide, gap_row, sems, wide_sem, gap_sem, *buffers = refs[2 * SPOTS :]
    core, x, z = place_of(here_ref[0])

    def copies(span):
        for spot in range(*SPANS[span]):
            column = pl.multiple_of(group_of(core, x, z, spot // SPOTS, spot % SPOTS) * GROUP, LANES)
            source = b_ref.at[:, pl.ds(column, GROUP)]
            place = (spot - SPANS[span][0]) * GROUP
            yield pltpu.make_async_copy(source, buffers[span].at[:, pl.ds(place, GROUP)], sems.at[spot])

    gap_copy = pltpu.make_async_copy(gap_ref, gap_row, gap_sem)
    gap_copy.start()
    first = pltpu.make_async_copy(b_ref.at[:, :PANEL], wide, wide_sem)
    first.start()
    for span in range(AHEAD):
        for copy in copies(span):
            copy.start()

    gap_copy.wait()
    gap = gap_row[...]
    moment = 0.15 * jnp.exp(jnp.full(gap.shape, laplace_ref[0], jnp.int32).astype(F32) * np.log(np.float32(1.5)))
    position = lax.broadcasted_iota(jnp.int32, gap.shape, 1)
    factor = jnp.where(position < live_ref[0, 0], jnp.exp(-(gap * moment) * 0.5), 0.0)
    f_ref[...] = jnp.broadcast_to(factor, (LANES, gap.shape[1])).T

    first.wait()
    for half, owner in enumerate((1 - core, core)):
        for c in range(0, HALF, LANES):
            piece = wide[:, pl.ds(pl.multiple_of(owner * HALF + c, LANES), LANES)].astype(F32)
            square = f_ref[...] * f_ref[...]
            panel[:, half * HALF + c : half * HALF + c + LANES] = (piece * square).astype(BF16)

    for span, (start, end) in enumerate(SPANS):
        for copy in copies(span):
            copy.wait()
        if span + AHEAD < len(SPANS):
            for copy in copies(span + AHEAD):
                copy.start()
        product = lax.dot_general(
            buffers[span][...], panel[...], (((0,), (0,)), ((), ())), preferred_element_type=F32
        ).astype(BF16)
        for spot in range(start, end):
            k, m = spot // SPOTS, spot % SPOTS
            rows = slice((spot - start) * GROUP, (spot - start + 1) * GROUP)
            theirs[m][k] = product[rows, :HALF]
            mine[k][m] = product[rows, HALF:]


def gram_parts(here, live, laplace, gap, bvals):
    rows = bvals.shape[0]
    part = jax.ShapeDtypeStruct((SPOTS, GROUP, HALF), BF16)
    return pl.pallas_call(
        gram_body,
        in_specs=[TABLE, TABLE, TABLE, FAR, FAR],
        out_specs=[WHOLE] * (2 * SPOTS + 1),
        out_shape=[part] * (2 * SPOTS) + [jax.ShapeDtypeStruct((rows, LANES), F32)],
        scratch_shapes=[
            pltpu.VMEM((rows, PANEL), BF16),
            pltpu.VMEM((rows, PANEL), BF16),
            pltpu.VMEM((1, rows), F32),
            pltpu.SemaphoreType.DMA((SPOTS * SPOTS,)),
            pltpu.SemaphoreType.DMA,
            pltpu.SemaphoreType.DMA,
        ]
        + [pltpu.VMEM((rows, (end - start) * GROUP), BF16) for start, end in SPANS],
        compiler_params=LARGE,
    )(here, live, laplace, gap, bvals)


BLOCKS = ((0, 128), (128, 384), (384, 768), (768, 1280), (1280, 1536))


def panel_body(here_ref, f_ref, b_ref, *refs):
    parts, (out_ref, gram, result, sems, out_sems, *buffers) = refs[: 4 * SPOTS // 2], refs[4 * SPOTS // 2 :]

    def copy(block):
        start, end = BLOCKS[block]
        return pltpu.make_async_copy(b_ref.at[pl.ds(start, end - start)], buffers[block], sems.at[block])

    def copy_out(block):
        start, end = BLOCKS[block]
        part = pl.ds(start, end - start)
        return pltpu.make_async_copy(result.at[part], out_ref.at[part], out_sems.at[block])

    for block in range(2):
        copy(block).start()
    core, x, z = place_of(here_ref[0])
    for whose, owner in enumerate((1 - core, core)):
        for k in range(SPOTS):
            for m in range(SPOTS):
                row = pl.multiple_of(group_of(owner, x, z, k, m) * GROUP, GROUP)
                column = pl.multiple_of(owner * HALF, HALF)
                gram[pl.ds(row, GROUP), pl.ds(column, HALF)] = parts[whose * SPOTS + k][m]
    for block, (start, end) in enumerate(BLOCKS):
        copy(block).wait()
        if block + 2 < len(BLOCKS):
            copy(block + 2).start()
        total = jnp.dot(buffers[block][...], gram[...], preferred_element_type=F32)
        for c in range(0, PANEL, LANES):
            result[start:end, c : c + LANES] = (total[:, c : c + LANES] * f_ref[start:end]).astype(BF16)
        copy_out(block).start()
    for block in range(len(BLOCKS)):
        copy_out(block).wait()


def panel_rows(here, bvals, factor, parts):
    rows, aux = bvals.shape
    return pl.pallas_call(
        panel_body,
        in_specs=[TABLE, WHOLE, FAR] + [WHOLE] * len(parts),
        out_specs=FAR,
        out_shape=jax.ShapeDtypeStruct((rows, PANEL), BF16),
        scratch_shapes=[
            pltpu.VMEM((aux, PANEL), BF16),
            pltpu.VMEM((rows, PANEL), BF16),
            pltpu.SemaphoreType.DMA((len(BLOCKS),)),
            pltpu.SemaphoreType.DMA((len(BLOCKS),)),
        ]
        + [pltpu.VMEM((end - start, aux), BF16) for start, end in BLOCKS],
        compiler_params=LARGE,
    )(here, factor, bvals, *parts)


def total_of(arrays):
    total = arrays[0].astype(F32)
    for array in arrays[1:]:
        total = total + array.astype(F32)
    return total


def on_device(bvals, gap, live, laplace):
    bvals = bvals[0]
    total_rows = bvals.shape[0] * lax.axis_size("rows")
    here = lax.axis_index("rows").reshape(1)
    parts = gram_parts(here, live, laplace, gap, bvals)
    theirs, mine, factor = parts[:SPOTS], parts[SPOTS : 2 * SPOTS], parts[-1]

    pairs = {k: total_of([mine[k], to_pair(theirs[k])]) for k in (1, 3, 2, 0)}
    held = total_of([pairs[0]] + [along_first(pairs[k].astype(BF16), k) for k in (1, 3, 2)])
    share = total_of([held[0]] + [along_second(held[k].astype(BF16), k) for k in (1, 3, 2)]).astype(BF16)
    whole = (total_of([across(share, 1), across(share, 0)]) / total_rows).astype(BF16)
    rows = {k: along_second(whole, SPOTS - k) for k in (1, 3, 2)}
    row = jnp.stack([whole] + [rows[k] for k in range(1, SPOTS)])
    own = {0: row, **{k: along_first(row, SPOTS - k) for k in (1, 3, 2)}}
    other = {k: to_pair(own[k]) for k in (0, 1, 3, 2)}
    parts = [other[k] for k in range(SPOTS)] + [own[k] for k in range(SPOTS)]
    return panel_rows(here, bvals, factor, parts)[None]


def solution(mesh):
    in_specs = (P("grp", "rows", None), P("grp", "rows"), P("grp", "rows"), P())
    out_specs = P("grp", "rows", None)
    return jax.shard_map(
        on_device, mesh=mesh, in_specs=in_specs, out_specs=out_specs, check_vma=False
    )
```

```python
import functools

import jax
import jax.numpy as jnp
import numpy as np
from jax import lax
from jax.experimental import pallas as pl
from jax.experimental.pallas import tpu as pltpu
from jax.sharding import PartitionSpec as P

PANEL = 512
HALF = 256
LANES = 128
SPOTS = 4
GROUP = 384
F32 = jnp.float32
BF16 = jnp.bfloat16
SIDES = (2, 2, SPOTS, SPOTS, 2)
NAMES = ("grp", "y", "z", "x", "core")


def shifted(array, steps):
    pairs = []
    for source in range(int(np.prod(SIDES))):
        spot = np.unravel_index(source, SIDES)
        step = steps[spot[-1]]
        goal = [(a + step.get(n, 0)) % s for a, n, s in zip(spot, NAMES, SIDES)]
        pairs.append((source, int(np.ravel_multi_index(goal, SIDES))))
    return lax.ppermute(array, ("grp", "rows"), pairs)


def along_first(array, step):
    return shifted(array, ({"x": step}, {"z": step}))


def along_second(array, step):
    return shifted(array, ({"z": step}, {"x": step}))


def to_pair(array):
    return shifted(array, ({"core": 1}, {"core": 1}))


def pair_in_two(array):
    return jnp.concatenate([to_pair(array[:2]), to_pair(array[2:])])


def across(array, step):
    return shifted(array, ({"grp": 1, "y": step},) * 2)


WHOLE = pl.BlockSpec(memory_space=pltpu.VMEM)
TABLE = pl.BlockSpec(memory_space=pltpu.SMEM)
FAR = pl.BlockSpec(memory_space=pltpu.HBM)
LARGE = pltpu.CompilerParams(vmem_limit_bytes=48 << 20)


def place_of(here):
    return here % 2, here // 2 % SPOTS, here // 8 % SPOTS


def group_of(core, x, z, k, m):
    by_x = jnp.where(core == 0, k, m)
    by_z = jnp.where(core == 0, m, k)
    return (x + by_x) % SPOTS * SPOTS + (z + by_z) % SPOTS


SPANS = ((0, 1), (1, 2), (2, 4), (4, 8), (8, 12), (12, 16))
AHEAD = 3


def gram_body(here_ref, live_ref, laplace_ref, gap_ref, b_ref, *refs):
    theirs, mine = refs[:SPOTS], refs[SPOTS : 2 * SPOTS]
    f_ref, panel, wide, gap_row, sems, wide_sem, gap_sem, *buffers = refs[2 * SPOTS :]
    core, x, z = place_of(here_ref[0])

    def copies(span):
        for spot in range(*SPANS[span]):
            column = pl.multiple_of(group_of(core, x, z, spot // SPOTS, spot % SPOTS) * GROUP, LANES)
            source = b_ref.at[:, pl.ds(column, GROUP)]
            place = (spot - SPANS[span][0]) * GROUP
            yield pltpu.make_async_copy(source, buffers[span].at[:, pl.ds(place, GROUP)], sems.at[spot])

    gap_copy = pltpu.make_async_copy(gap_ref, gap_row, gap_sem)
    gap_copy.start()
    first = pltpu.make_async_copy(b_ref.at[:, :PANEL], wide, wide_sem)
    first.start()
    for span in range(AHEAD):
        for copy in copies(span):
            copy.start()

    gap_copy.wait()
    gap = gap_row[...]
    moment = 0.15 * jnp.exp(jnp.full(gap.shape, laplace_ref[0], jnp.int32).astype(F32) * np.log(np.float32(1.5)))
    position = lax.broadcasted_iota(jnp.int32, gap.shape, 1)
    factor = jnp.where(position < live_ref[0, 0], jnp.exp(-(gap * moment) * 0.5), 0.0)
    f_ref[...] = jnp.broadcast_to(factor, (LANES, gap.shape[1])).T

    first.wait()
    for half, owner in enumerate((1 - core, core)):
        for c in range(0, HALF, LANES):
            piece = wide[:, pl.ds(pl.multiple_of(owner * HALF + c, LANES), LANES)].astype(F32)
            square = f_ref[...] * f_ref[...]
            panel[:, half * HALF + c : half * HALF + c + LANES] = (piece * square).astype(BF16)

    for span, (start, end) in enumerate(SPANS):
        for copy in copies(span):
            copy.wait()
        if span + AHEAD < len(SPANS):
            for copy in copies(span + AHEAD):
                copy.start()
        product = lax.dot_general(
            buffers[span][...], panel[...], (((0,), (0,)), ((), ())), preferred_element_type=F32
        ).astype(BF16)
        for spot in range(start, end):
            k, m = spot // SPOTS, spot % SPOTS
            rows = slice((spot - start) * GROUP, (spot - start + 1) * GROUP)
            theirs[m][k] = product[rows, :HALF]
            mine[k][m] = product[rows, HALF:]


def gram_parts(here, live, laplace, gap, bvals):
    rows = bvals.shape[0]
    part = jax.ShapeDtypeStruct((SPOTS, GROUP, HALF), BF16)
    return pl.pallas_call(
        gram_body,
        in_specs=[TABLE, TABLE, TABLE, FAR, FAR],
        out_specs=[WHOLE] * (2 * SPOTS + 1),
        out_shape=[part] * (2 * SPOTS) + [jax.ShapeDtypeStruct((rows, LANES), F32)],
        scratch_shapes=[
            pltpu.VMEM((rows, PANEL), BF16),
            pltpu.VMEM((rows, PANEL), BF16),
            pltpu.VMEM((1, rows), F32),
            pltpu.SemaphoreType.DMA((SPOTS * SPOTS,)),
            pltpu.SemaphoreType.DMA,
            pltpu.SemaphoreType.DMA,
        ]
        + [pltpu.VMEM((rows, (end - start) * GROUP), BF16) for start, end in SPANS],
        compiler_params=LARGE,
    )(here, live, laplace, gap, bvals)


BLOCKS = ((0, 128), (128, 384), (384, 768), (768, 1280), (1280, 1536))


def panel_body(steps, here_ref, b_ref, *refs):
    count = 2 * len(steps)
    parts, refs = refs[:count], refs[count:]
    is_last = len(steps) > 1
    if is_last:
        before_ref, f_ref, out_ref, before, result, before_sems, out_sems = refs
        held = b_ref
    else:
        out_ref, zero_ref, held, result, sems, out_sems = refs
        zero_ref[...] = jnp.zeros_like(zero_ref)

    def copy(block):
        start, end = BLOCKS[block]
        part = pl.ds(start, end - start)
        return pltpu.make_async_copy(b_ref.at[part], held.at[part], sems.at[block])

    def copy_before(block):
        start, end = BLOCKS[block]
        part = pl.ds(start, end - start)
        return pltpu.make_async_copy(before_ref.at[part], before.at[part], before_sems.at[block])

    def copy_out(block):
        start, end = BLOCKS[block]
        part = pl.ds(start, end - start)
        return pltpu.make_async_copy(result.at[part], out_ref.at[part], out_sems.at[block])

    def begin(block):
        (copy_before if is_last else copy)(block).start()

    for block in range(2):
        begin(block)
    core, x, z = place_of(here_ref[0])
    for block, (start, end) in enumerate(BLOCKS):
        (copy_before if is_last else copy)(block).wait()
        if block + 2 < len(BLOCKS):
            begin(block + 2)
        for whose, owner in enumerate((1 - core, core)):
            total = before[start:end, whose * HALF : (whose + 1) * HALF] if is_last else None
            for n, k in enumerate(steps):
                columns = [
                    held[start:end, pl.ds(pl.multiple_of(group_of(owner, x, z, k, m) * GROUP, GROUP), GROUP)]
                    for m in range(SPOTS)
                ]
                right = parts[whose * len(steps) + n][...].reshape(SPOTS * GROUP, HALF)
                product = jnp.dot(jnp.concatenate(columns, axis=1), right, preferred_element_type=F32)
                total = product if total is None else total + product
            if is_last:
                for c in range(0, HALF, LANES):
                    column = pl.multiple_of(owner * HALF + c, LANES)
                    piece = total[:, c : c + LANES] * f_ref[start:end]
                    result[start:end, pl.ds(column, LANES)] = piece.astype(BF16)
            else:
                result[start:end, whose * HALF : (whose + 1) * HALF] = total
        copy_out(block).start()
    for block in range(len(BLOCKS)):
        copy_out(block).wait()


def panel_part(steps, here, bvals, parts, before=None, factor=None):
    rows, aux = bvals.shape
    is_last = before is not None
    blocks = pltpu.SemaphoreType.DMA((len(BLOCKS),))
    kind = BF16 if is_last else F32
    shape = jax.ShapeDtypeStruct((rows, PANEL), kind) if is_last else pltpu.HBM((rows, PANEL), kind)
    zeros = jax.ShapeDtypeStruct((SPOTS, GROUP, HALF), BF16)
    return pl.pallas_call(
        functools.partial(panel_body, steps),
        in_specs=[TABLE, WHOLE if is_last else FAR] + [WHOLE] * len(parts) + [FAR, WHOLE] * is_last,
        out_specs=FAR if is_last else [FAR, WHOLE, WHOLE],
        out_shape=shape if is_last else [shape, zeros, pltpu.VMEM((rows, aux), BF16)],
        scratch_shapes=[pltpu.VMEM((rows, PANEL), F32)] * is_last
        + [pltpu.VMEM((rows, PANEL), kind), blocks, blocks],
        compiler_params=pltpu.CompilerParams(vmem_limit_bytes=16 << 20),
        cost_estimate=pl.CostEstimate(flops=0, bytes_accessed=0, transcendentals=0),
    )(here, bvals, *parts, *([before, factor] if is_last else []))


def total_of(arrays):
    total = arrays[0].astype(F32)
    for array in arrays[1:]:
        total = total + array.astype(F32)
    return total


def on_device(bvals, gap, live, laplace):
    bvals = bvals[0]
    total_rows = bvals.shape[0] * lax.axis_size("rows")
    here = lax.axis_index("rows").reshape(1)
    parts = gram_parts(here, live, laplace, gap, bvals)
    theirs, mine, factor = parts[:SPOTS], parts[SPOTS : 2 * SPOTS], parts[-1]

    pairs = {k: total_of([mine[k], to_pair(theirs[k])]) for k in (1, 3, 2, 0)}
    held = total_of([pairs[0]] + [along_first(pairs[k].astype(BF16), k) for k in (1, 3, 2)])
    share = total_of([held[0]] + [along_second(held[k].astype(BF16), k) for k in (1, 3, 2)]).astype(BF16)
    whole = (total_of([across(share, 1), across(share, 0)]) / total_rows).astype(BF16)
    rows = {k: along_second(whole, SPOTS - k) for k in (1, 3, 2)}
    row = jnp.stack([whole] + [rows[k] for k in range(1, SPOTS)])
    own = {k: along_first(row, SPOTS - k) for k in (3, 1, 2)}
    result, zeros, bvals = panel_part((0,), here, bvals, [to_pair(row), row])
    own[3] = own[3] + zeros
    other = {3: to_pair(own[3])}
    for k in (1, 2):
        own[k] = own[k] + BF16(0.0) * other[3]
        other[k] = pair_in_two(own[k])
    parts = [other[k] for k in (3, 1, 2)] + [own[k] for k in (3, 1, 2)]
    return panel_part((3, 1, 2), here, bvals, parts, result, factor)[None]


def solution(mesh):
    in_specs = (P("grp", "rows", None), P("grp", "rows"), P("grp", "rows"), P())
    out_specs = P("grp", "rows", None)
    return jax.shard_map(
        on_device, mesh=mesh, in_specs=in_specs, out_specs=out_specs, check_vma=False
    )
```

```python
import functools

import jax
import jax.numpy as jnp
import numpy as np
from jax import lax
from jax.experimental import pallas as pl
from jax.experimental.pallas import tpu as pltpu
from jax.sharding import PartitionSpec as P

PANEL = 512
HALF = 256
LANES = 128
SPOTS = 4
GROUP = 384
F32 = jnp.float32
BF16 = jnp.bfloat16
SIDES = (2, 2, SPOTS, SPOTS, 2)
NAMES = ("grp", "y", "z", "x", "core")


def shifted(array, steps):
    pairs = []
    for source in range(int(np.prod(SIDES))):
        spot = np.unravel_index(source, SIDES)
        step = steps[spot[-1]]
        goal = [(a + step.get(n, 0)) % s for a, n, s in zip(spot, NAMES, SIDES)]
        pairs.append((source, int(np.ravel_multi_index(goal, SIDES))))
    return lax.ppermute(array, ("grp", "rows"), pairs)


def along_first(array, step):
    return shifted(array, ({"x": step}, {"z": step}))


def along_second(array, step):
    return shifted(array, ({"z": step}, {"x": step}))


def to_pair(array):
    return shifted(array, ({"core": 1}, {"core": 1}))


def across(array, step):
    return shifted(array, ({"grp": 1, "y": step},) * 2)


WHOLE = pl.BlockSpec(memory_space=pltpu.VMEM)
TABLE = pl.BlockSpec(memory_space=pltpu.SMEM)
FAR = pl.BlockSpec(memory_space=pltpu.HBM)
LARGE = pltpu.CompilerParams(vmem_limit_bytes=48 << 20)


def place_of(here):
    return here % 2, here // 2 % SPOTS, here // 8 % SPOTS


def group_of(core, x, z, k, m):
    by_x = jnp.where(core == 0, k, m)
    by_z = jnp.where(core == 0, m, k)
    return (x + by_x) % SPOTS * SPOTS + (z + by_z) % SPOTS


SPANS = ((0, 1), (1, 2), (2, 4), (4, 8), (8, 12), (12, 16))
AHEAD = 3


def gram_body(here_ref, live_ref, laplace_ref, gap_ref, b_ref, *refs):
    theirs, mine = refs[:SPOTS], refs[SPOTS : 2 * SPOTS]
    f_ref, panel, wide, gap_row, sems, wide_sem, gap_sem, *buffers = refs[2 * SPOTS :]
    core, x, z = place_of(here_ref[0])

    def copies(span):
        for spot in range(*SPANS[span]):
            column = pl.multiple_of(group_of(core, x, z, spot // SPOTS, spot % SPOTS) * GROUP, LANES)
            source = b_ref.at[:, pl.ds(column, GROUP)]
            place = (spot - SPANS[span][0]) * GROUP
            yield pltpu.make_async_copy(source, buffers[span].at[:, pl.ds(place, GROUP)], sems.at[spot])

    gap_copy = pltpu.make_async_copy(gap_ref, gap_row, gap_sem)
    gap_copy.start()
    first = pltpu.make_async_copy(b_ref.at[:, :PANEL], wide, wide_sem)
    first.start()
    for span in range(AHEAD):
        for copy in copies(span):
            copy.start()

    gap_copy.wait()
    gap = gap_row[...]
    moment = 0.15 * jnp.exp(jnp.full(gap.shape, laplace_ref[0], jnp.int32).astype(F32) * np.log(np.float32(1.5)))
    position = lax.broadcasted_iota(jnp.int32, gap.shape, 1)
    factor = jnp.where(position < live_ref[0, 0], jnp.exp(-(gap * moment) * 0.5), 0.0)
    f_ref[...] = jnp.broadcast_to(factor, (LANES, gap.shape[1])).T

    first.wait()
    for half, owner in enumerate((1 - core, core)):
        for c in range(0, HALF, LANES):
            piece = wide[:, pl.ds(pl.multiple_of(owner * HALF + c, LANES), LANES)].astype(F32)
            square = f_ref[...] * f_ref[...]
            panel[:, half * HALF + c : half * HALF + c + LANES] = (piece * square).astype(BF16)

    for span, (start, end) in enumerate(SPANS):
        for copy in copies(span):
            copy.wait()
        if span + AHEAD < len(SPANS):
            for copy in copies(span + AHEAD):
                copy.start()
        product = lax.dot_general(
            buffers[span][...], panel[...], (((0,), (0,)), ((), ())), preferred_element_type=F32
        ).astype(BF16)
        for spot in range(start, end):
            k, m = spot // SPOTS, spot % SPOTS
            rows = slice((spot - start) * GROUP, (spot - start + 1) * GROUP)
            theirs[m][k] = product[rows, :HALF]
            mine[k][m] = product[rows, HALF:]


def gram_parts(here, live, laplace, gap, bvals):
    rows = bvals.shape[0]
    part = jax.ShapeDtypeStruct((SPOTS, GROUP, HALF), BF16)
    return pl.pallas_call(
        gram_body,
        in_specs=[TABLE, TABLE, TABLE, FAR, FAR],
        out_specs=[WHOLE] * (2 * SPOTS + 1),
        out_shape=[part] * (2 * SPOTS) + [jax.ShapeDtypeStruct((rows, LANES), F32)],
        scratch_shapes=[
            pltpu.VMEM((rows, PANEL), BF16),
            pltpu.VMEM((rows, PANEL), BF16),
            pltpu.VMEM((1, rows), F32),
            pltpu.SemaphoreType.DMA((SPOTS * SPOTS,)),
            pltpu.SemaphoreType.DMA,
            pltpu.SemaphoreType.DMA,
        ]
        + [pltpu.VMEM((rows, (end - start) * GROUP), BF16) for start, end in SPANS],
        compiler_params=LARGE,
    )(here, live, laplace, gap, bvals)


BLOCKS = ((0, 128), (128, 384), (384, 768), (768, 1280), (1280, 1536))
HALVES = ((0, 1024), (1024, 1536))


def early_body(here_ref, b_ref, other_ref, own_ref, out_ref, zero_ref, held, result, sems, out_sems):
    zero_ref[...] = jnp.zeros_like(zero_ref)

    def copy(block):
        start, end = BLOCKS[block]
        part = pl.ds(start, end - start)
        return pltpu.make_async_copy(b_ref.at[part], held.at[part], sems.at[block])

    def copy_out(block):
        start, end = BLOCKS[block]
        part = pl.ds(start, end - start)
        return pltpu.make_async_copy(result.at[part], out_ref.at[part], out_sems.at[block])

    for block in range(2):
        copy(block).start()
    core, x, z = place_of(here_ref[0])
    for block, (start, end) in enumerate(BLOCKS):
        copy(block).wait()
        if block + 2 < len(BLOCKS):
            copy(block + 2).start()
        for whose, (owner, part) in enumerate(((1 - core, other_ref), (core, own_ref))):
            left = columns_of(held, start, end, owner, x, z, 0)
            product = jnp.dot(left, part[...].reshape(SPOTS * GROUP, HALF), preferred_element_type=F32)
            result[start:end, whose * HALF : (whose + 1) * HALF] = product
        copy_out(block).start()
    for block in range(len(BLOCKS)):
        copy_out(block).wait()


def columns_of(held, start, end, owner, x, z, k):
    columns = []
    for m in range(SPOTS):
        column = pl.multiple_of(group_of(owner, x, z, k, m) * GROUP, GROUP)
        columns.append(held[start:end, pl.ds(column, GROUP)])
    return jnp.concatenate(columns, axis=1)


def early_panel(here, bvals, other, own):
    rows, aux = bvals.shape
    blocks = pltpu.SemaphoreType.DMA((len(BLOCKS),))
    return pl.pallas_call(
        early_body,
        in_specs=[TABLE, FAR, WHOLE, WHOLE],
        out_specs=[FAR, WHOLE, WHOLE],
        out_shape=[
            pltpu.HBM((rows, PANEL), F32),
            jax.ShapeDtypeStruct((SPOTS, GROUP, HALF), BF16),
            pltpu.VMEM((rows, aux), BF16),
        ],
        scratch_shapes=[pltpu.VMEM((rows, PANEL), F32), blocks, blocks],
        compiler_params=MODEST,
        cost_estimate=SMALL,
    )(here, bvals, other, own)


MODEST = pltpu.CompilerParams(vmem_limit_bytes=16 << 20)
SMALL = pl.CostEstimate(flops=0, bytes_accessed=0, transcendentals=0)


def late_body(steps, whose, here_ref, held, before_ref, f_ref, *refs):
    parts, (out_ref, before, result, sems, out_sems) = refs[: len(steps)], refs[-5:]
    core, x, z = place_of(here_ref[0])
    owner = core if whose else 1 - core

    def copy(block):
        start, end = HALVES[block]
        part = pl.ds(start, end - start)
        source = before_ref.at[part, pl.ds(whose * HALF, HALF)]
        return pltpu.make_async_copy(source, before.at[part], sems.at[block])

    def copy_out(block):
        start, end = HALVES[block]
        part = pl.ds(start, end - start)
        target = out_ref.at[part, pl.ds(pl.multiple_of(owner * HALF, HALF), HALF)]
        return pltpu.make_async_copy(result.at[part], target, out_sems.at[block])

    for block in range(len(HALVES)):
        copy(block).start()
    for block, (start, end) in enumerate(HALVES):
        middle = (start + end) // 2
        spans = ((start, middle), (middle, end))
        totals = [None, None]
        for part, k in zip(parts, steps):
            right = part[...].reshape(SPOTS * GROUP, HALF)
            for n, (low, high) in enumerate(spans):
                left = columns_of(held, low, high, owner, x, z, k)
                product = jnp.dot(left, right, preferred_element_type=F32)
                totals[n] = product if totals[n] is None else totals[n] + product
        copy(block).wait()
        for total, (low, high) in zip(totals, spans):
            for c in range(0, HALF, LANES):
                piece = total[:, c : c + LANES] + before[low:high, c : c + LANES]
                result[low:high, c : c + LANES] = (piece * f_ref[low:high]).astype(BF16)
        copy_out(block).start()
    for block in range(len(HALVES)):
        copy_out(block).wait()


def late_panel(steps, whose, here, held, before, factor, parts, out):
    rows = held.shape[0]
    blocks = pltpu.SemaphoreType.DMA((len(HALVES),))
    extra = [] if out is None else [out]
    return pl.pallas_call(
        functools.partial(late_body, steps, whose),
        in_specs=[TABLE, WHOLE, FAR, WHOLE] + [WHOLE] * len(parts) + [FAR] * len(extra),
        out_specs=FAR,
        out_shape=jax.ShapeDtypeStruct((rows, PANEL), BF16),
        scratch_shapes=[pltpu.VMEM((rows, HALF), F32), pltpu.VMEM((rows, HALF), BF16), blocks, blocks],
        input_output_aliases={4 + len(parts): 0} if extra else {},
        compiler_params=MODEST,
        cost_estimate=SMALL,
    )(here, held, before, factor, *parts, *extra)


def total_of(arrays):
    total = arrays[0].astype(F32)
    for array in arrays[1:]:
        total = total + array.astype(F32)
    return total


def on_device(bvals, gap, live, laplace):
    bvals = bvals[0]
    total_rows = bvals.shape[0] * lax.axis_size("rows")
    here = lax.axis_index("rows").reshape(1)
    parts = gram_parts(here, live, laplace, gap, bvals)
    theirs, mine, factor = parts[:SPOTS], parts[SPOTS : 2 * SPOTS], parts[-1]

    pairs = {k: total_of([mine[k], to_pair(theirs[k])]) for k in (1, 3, 2, 0)}
    held = total_of([pairs[0]] + [along_first(pairs[k].astype(BF16), k) for k in (1, 3, 2)])
    share = total_of([held[0]] + [along_second(held[k].astype(BF16), k) for k in (1, 3, 2)]).astype(BF16)
    whole = (total_of([across(share, 1), across(share, 0)]) / total_rows).astype(BF16)
    rows = {k: along_second(whole, SPOTS - k) for k in (1, 3, 2)}
    row = jnp.stack([whole] + [rows[k] for k in range(1, SPOTS)])
    own = {k: along_first(row, SPOTS - k) for k in (3, 1, 2)}
    early, zeros, held = early_panel(here, bvals, to_pair(row), row)
    own[3] = own[3] + zeros
    other = {3: to_pair(own[3])}
    for k in (1, 2):
        own[k] = own[k] + BF16(0.0) * other[3]
        other[k] = to_pair(own[k])
    result, steps = None, (3, 1, 2)
    for whose, parts in ((1, own), (0, other)):
        result = late_panel(steps, whose, here, held, early, factor, [parts[k] for k in steps], result)
    return result[None]


def solution(mesh):
    in_specs = (P("grp", "rows", None), P("grp", "rows"), P("grp", "rows"), P())
    out_specs = P("grp", "rows", None)
    return jax.shard_map(
        on_device, mesh=mesh, in_specs=in_specs, out_specs=out_specs, check_vma=False
    )
```

```python
import functools

import jax
import jax.numpy as jnp
import numpy as np
from jax import lax
from jax.experimental import pallas as pl
from jax.experimental.pallas import tpu as pltpu
from jax.sharding import PartitionSpec as P

PANEL = 512
HALF = 256
LANES = 128
SPOTS = 4
GROUP = 384
F32 = jnp.float32
BF16 = jnp.bfloat16
SIDES = (2, 2, SPOTS, SPOTS, 2)
NAMES = ("grp", "y", "z", "x", "core")


def shifted(array, steps):
    pairs = []
    for source in range(int(np.prod(SIDES))):
        spot = np.unravel_index(source, SIDES)
        step = steps[spot[-1]]
        goal = [(a + step.get(n, 0)) % s for a, n, s in zip(spot, NAMES, SIDES)]
        pairs.append((source, int(np.ravel_multi_index(goal, SIDES))))
    return lax.ppermute(array, ("grp", "rows"), pairs)


def along_first(array, step):
    return shifted(array, ({"x": step}, {"z": step}))


def along_second(array, step):
    return shifted(array, ({"z": step}, {"x": step}))


def to_pair(array):
    return shifted(array, ({"core": 1}, {"core": 1}))


def across(array, step):
    return shifted(array, ({"grp": 1, "y": step},) * 2)


WHOLE = pl.BlockSpec(memory_space=pltpu.VMEM)
TABLE = pl.BlockSpec(memory_space=pltpu.SMEM)
FAR = pl.BlockSpec(memory_space=pltpu.HBM)
LARGE = pltpu.CompilerParams(vmem_limit_bytes=48 << 20)


def place_of(here):
    return here % 2, here // 2 % SPOTS, here // 8 % SPOTS


def group_of(core, x, z, k, m):
    by_x = jnp.where(core == 0, k, m)
    by_z = jnp.where(core == 0, m, k)
    return (x + by_x) % SPOTS * SPOTS + (z + by_z) % SPOTS


SPANS = ((0, 1), (1, 2), (2, 4), (4, 8), (8, 12), (12, 16))
AHEAD = 3


def gram_body(here_ref, live_ref, laplace_ref, gap_ref, b_ref, *refs):
    theirs, mine = refs[:SPOTS], refs[SPOTS : 2 * SPOTS]
    f_ref, panel, wide, gap_row, sems, wide_sem, gap_sem, *buffers = refs[2 * SPOTS :]
    core, x, z = place_of(here_ref[0])

    def copies(span):
        for spot in range(*SPANS[span]):
            column = pl.multiple_of(group_of(core, x, z, spot // SPOTS, spot % SPOTS) * GROUP, LANES)
            source = b_ref.at[:, pl.ds(column, GROUP)]
            place = (spot - SPANS[span][0]) * GROUP
            yield pltpu.make_async_copy(source, buffers[span].at[:, pl.ds(place, GROUP)], sems.at[spot])

    gap_copy = pltpu.make_async_copy(gap_ref, gap_row, gap_sem)
    gap_copy.start()
    first = pltpu.make_async_copy(b_ref.at[:, :PANEL], wide, wide_sem)
    first.start()
    for span in range(AHEAD):
        for copy in copies(span):
            copy.start()

    gap_copy.wait()
    gap = gap_row[...]
    moment = 0.15 * jnp.exp(jnp.full(gap.shape, laplace_ref[0], jnp.int32).astype(F32) * np.log(np.float32(1.5)))
    position = lax.broadcasted_iota(jnp.int32, gap.shape, 1)
    factor = jnp.where(position < live_ref[0, 0], jnp.exp(-(gap * moment) * 0.5), 0.0)
    f_ref[...] = jnp.broadcast_to(factor, (LANES, gap.shape[1])).T

    first.wait()
    for half, owner in enumerate((1 - core, core)):
        for c in range(0, HALF, LANES):
            piece = wide[:, pl.ds(pl.multiple_of(owner * HALF + c, LANES), LANES)].astype(F32)
            square = f_ref[...] * f_ref[...]
            panel[:, half * HALF + c : half * HALF + c + LANES] = (piece * square).astype(BF16)

    for span, (start, end) in enumerate(SPANS):
        for copy in copies(span):
            copy.wait()
        if span + AHEAD < len(SPANS):
            for copy in copies(span + AHEAD):
                copy.start()
        product = lax.dot_general(
            buffers[span][...], panel[...], (((0,), (0,)), ((), ())), preferred_element_type=F32
        ).astype(BF16)
        for spot in range(start, end):
            k, m = spot // SPOTS, spot % SPOTS
            rows = slice((spot - start) * GROUP, (spot - start + 1) * GROUP)
            theirs[m][k] = product[rows, :HALF]
            mine[k][m] = product[rows, HALF:]


def gram_parts(here, live, laplace, gap, bvals):
    rows = bvals.shape[0]
    part = jax.ShapeDtypeStruct((SPOTS, GROUP, HALF), BF16)
    return pl.pallas_call(
        gram_body,
        in_specs=[TABLE, TABLE, TABLE, FAR, FAR],
        out_specs=[WHOLE] * (2 * SPOTS + 1),
        out_shape=[part] * (2 * SPOTS) + [jax.ShapeDtypeStruct((rows, LANES), F32)],
        scratch_shapes=[
            pltpu.VMEM((rows, PANEL), BF16),
            pltpu.VMEM((rows, PANEL), BF16),
            pltpu.VMEM((1, rows), F32),
            pltpu.SemaphoreType.DMA((SPOTS * SPOTS,)),
            pltpu.SemaphoreType.DMA,
            pltpu.SemaphoreType.DMA,
        ]
        + [pltpu.VMEM((rows, (end - start) * GROUP), BF16) for start, end in SPANS],
        compiler_params=LARGE,
    )(here, live, laplace, gap, bvals)


BLOCKS = ((0, 128), (128, 384), (384, 768), (768, 1280), (1280, 1536))
HALVES = ((0, 1024), (1024, 1536))


def early_body(here_ref, b_ref, other_ref, own_ref, out_ref, zero_ref, held, result, sems, out_sems):
    zero_ref[...] = jnp.zeros_like(zero_ref)

    def copy(block):
        start, end = BLOCKS[block]
        part = pl.ds(start, end - start)
        return pltpu.make_async_copy(b_ref.at[part], held.at[part], sems.at[block])

    def copy_out(block):
        start, end = BLOCKS[block]
        part = pl.ds(start, end - start)
        return pltpu.make_async_copy(result.at[part], out_ref.at[part], out_sems.at[block])

    for block in range(2):
        copy(block).start()
    core, x, z = place_of(here_ref[0])
    for block, (start, end) in enumerate(BLOCKS):
        copy(block).wait()
        if block + 2 < len(BLOCKS):
            copy(block + 2).start()
        for whose, (owner, part) in enumerate(((1 - core, other_ref), (core, own_ref))):
            left = columns_of(held, start, end, owner, x, z, 0)
            product = jnp.dot(left, part[...].reshape(SPOTS * GROUP, HALF), preferred_element_type=F32)
            result[start:end, whose * HALF : (whose + 1) * HALF] = product
        copy_out(block).start()
    for block in range(len(BLOCKS)):
        copy_out(block).wait()


def columns_of(held, start, end, owner, x, z, k):
    columns = []
    for m in range(SPOTS):
        column = pl.multiple_of(group_of(owner, x, z, k, m) * GROUP, GROUP)
        columns.append(held[start:end, pl.ds(column, GROUP)])
    return jnp.concatenate(columns, axis=1)


def early_panel(here, bvals, other, own):
    rows, aux = bvals.shape
    blocks = pltpu.SemaphoreType.DMA((len(BLOCKS),))
    return pl.pallas_call(
        early_body,
        in_specs=[TABLE, FAR, WHOLE, WHOLE],
        out_specs=[FAR, WHOLE, WHOLE],
        out_shape=[
            pltpu.HBM((rows, PANEL), F32),
            jax.ShapeDtypeStruct((SPOTS, GROUP, HALF), BF16),
            pltpu.VMEM((rows, aux), BF16),
        ],
        scratch_shapes=[pltpu.VMEM((rows, PANEL), F32), blocks, blocks],
        compiler_params=MODEST,
        cost_estimate=SMALL,
    )(here, bvals, other, own)


MODEST = pltpu.CompilerParams(vmem_limit_bytes=16 << 20)
SMALL = pl.CostEstimate(flops=0, bytes_accessed=0, transcendentals=0)


def late_body(steps, whose, is_last, here_ref, held, before_ref, f_ref, *refs):
    parts, (out_ref, before, result, sems, out_sems) = refs[: len(steps)], refs[-5:]
    if not is_last:
        out_ref, zero_ref = refs[len(steps) : len(steps) + 2]
        zero_ref[...] = jnp.zeros_like(zero_ref)
    core, x, z = place_of(here_ref[0])
    owner = core if whose else 1 - core

    def copy(block):
        start, end = HALVES[block]
        part = pl.ds(start, end - start)
        source = before_ref.at[part, pl.ds(whose * HALF if before_ref.shape[1] == PANEL else 0, HALF)]
        return pltpu.make_async_copy(source, before.at[part], sems.at[block])

    def copy_out(block):
        start, end = HALVES[block]
        part = pl.ds(start, end - start)
        target = out_ref.at[part]
        if is_last:
            target = out_ref.at[part, pl.ds(pl.multiple_of(owner * HALF, HALF), HALF)]
        return pltpu.make_async_copy(result.at[part], target, out_sems.at[block])

    for block in range(len(HALVES)):
        copy(block).start()
    for block, (start, end) in enumerate(HALVES):
        middle = (start + end) // 2
        spans = ((start, middle), (middle, end))
        totals = [None, None]
        for part, k in zip(parts, steps):
            right = part[...].reshape(SPOTS * GROUP, HALF)
            for n, (low, high) in enumerate(spans):
                left = columns_of(held, low, high, owner, x, z, k)
                product = jnp.dot(left, right, preferred_element_type=F32)
                totals[n] = product if totals[n] is None else totals[n] + product
        copy(block).wait()
        for total, (low, high) in zip(totals, spans):
            for c in range(0, HALF, LANES):
                piece = total[:, c : c + LANES] + before[low:high, c : c + LANES]
                result[low:high, c : c + LANES] = (piece * f_ref[low:high]).astype(BF16) if is_last else piece
        copy_out(block).start()
    for block in range(len(HALVES)):
        copy_out(block).wait()


def late_panel(steps, whose, here, held, before, factor, parts, out, is_last=True):
    rows = held.shape[0]
    kind = BF16 if is_last else F32
    blocks = pltpu.SemaphoreType.DMA((len(HALVES),))
    extra = [] if out is None else [out]
    return pl.pallas_call(
        functools.partial(late_body, steps, whose, is_last),
        in_specs=[TABLE, WHOLE, FAR, WHOLE] + [WHOLE] * len(parts) + [FAR] * len(extra),
        out_specs=[FAR] + [WHOLE] * (not is_last),
        out_shape=[jax.ShapeDtypeStruct((rows, PANEL), BF16)]
        if is_last
        else [pltpu.HBM((rows, HALF), F32), jax.ShapeDtypeStruct(parts[0].shape, BF16)],
        scratch_shapes=[pltpu.VMEM((rows, HALF), F32), pltpu.VMEM((rows, HALF), kind), blocks, blocks],
        input_output_aliases={4 + len(parts): 0} if extra else {},
        compiler_params=MODEST,
        cost_estimate=SMALL,
    )(here, held, before, factor, *parts, *extra)


def total_of(arrays):
    total = arrays[0].astype(F32)
    for array in arrays[1:]:
        total = total + array.astype(F32)
    return total


def on_device(bvals, gap, live, laplace):
    bvals = bvals[0]
    total_rows = bvals.shape[0] * lax.axis_size("rows")
    here = lax.axis_index("rows").reshape(1)
    parts = gram_parts(here, live, laplace, gap, bvals)
    theirs, mine, factor = parts[:SPOTS], parts[SPOTS : 2 * SPOTS], parts[-1]

    pairs = {k: total_of([mine[k], to_pair(theirs[k])]) for k in (1, 3, 2, 0)}
    held = total_of([pairs[0]] + [along_first(pairs[k].astype(BF16), k) for k in (1, 3, 2)])
    share = total_of([held[0]] + [along_second(held[k].astype(BF16), k) for k in (1, 3, 2)]).astype(BF16)
    whole = (total_of([across(share, 1), across(share, 0)]) / total_rows).astype(BF16)
    rows = {k: along_second(whole, SPOTS - k) for k in (1, 3, 2)}
    row = jnp.stack([whole] + [rows[k] for k in range(1, SPOTS)])
    own = {k: along_first(row, SPOTS - k) for k in (3, 1, 2)}
    early, zeros, held = early_panel(here, bvals, to_pair(row), row)
    own[3] = own[3] + zeros
    other = {3: to_pair(own[3])}
    middle, zeros = late_panel((3,), 1, here, held, early, factor, [own[3]], None, False)
    for k in (1, 2):
        own[k] = own[k] + (zeros + BF16(0.0) * other[3])
        other[k] = to_pair(own[k])
    (result,) = late_panel((1, 2), 1, here, held, middle, factor, [own[k] for k in (1, 2)], None)
    (result,) = late_panel((3, 1, 2), 0, here, held, early, factor, [other[k] for k in (3, 1, 2)], result)
    return result[None]


def solution(mesh):
    in_specs = (P("grp", "rows", None), P("grp", "rows"), P("grp", "rows"), P())
    out_specs = P("grp", "rows", None)
    return jax.shard_map(
        on_device, mesh=mesh, in_specs=in_specs, out_specs=out_specs, check_vma=False
    )
```

```python
import functools

import jax
import jax.numpy as jnp
import numpy as np
from jax import lax
from jax.experimental import pallas as pl
from jax.experimental.pallas import tpu as pltpu
from jax.sharding import PartitionSpec as P

PANEL = 512
HALF = 256
LANES = 128
SPOTS = 4
GROUP = 384
F32 = jnp.float32
BF16 = jnp.bfloat16
SIDES = (2, 2, SPOTS, SPOTS, 2)
NAMES = ("grp", "y", "z", "x", "core")


def shifted(array, steps):
    pairs = []
    for source in range(int(np.prod(SIDES))):
        spot = np.unravel_index(source, SIDES)
        step = steps[spot[-1]]
        goal = [(a + step.get(n, 0)) % s for a, n, s in zip(spot, NAMES, SIDES)]
        pairs.append((source, int(np.ravel_multi_index(goal, SIDES))))
    return lax.ppermute(array, ("grp", "rows"), pairs)


def along_first(array, step):
    return shifted(array, ({"x": step}, {"z": step}))


def along_second(array, step):
    return shifted(array, ({"z": step}, {"x": step}))


def to_pair(array):
    return shifted(array, ({"core": 1}, {"core": 1}))


def across(array, step):
    return shifted(array, ({"grp": 1, "y": step},) * 2)


WHOLE = pl.BlockSpec(memory_space=pltpu.VMEM)
TABLE = pl.BlockSpec(memory_space=pltpu.SMEM)
FAR = pl.BlockSpec(memory_space=pltpu.HBM)
LARGE = pltpu.CompilerParams(vmem_limit_bytes=48 << 20)


def place_of(here):
    return here % 2, here // 2 % SPOTS, here // 8 % SPOTS


def group_of(core, x, z, k, m):
    by_x = jnp.where(core == 0, k, m)
    by_z = jnp.where(core == 0, m, k)
    return (x + by_x) % SPOTS * SPOTS + (z + by_z) % SPOTS


SPANS = ((0, 1), (1, 2), (2, 4), (4, 8), (8, 12), (12, 16))
AHEAD = 3


def gram_body(here_ref, live_ref, laplace_ref, gap_ref, b_ref, *refs):
    theirs, mine = refs[:SPOTS], refs[SPOTS : 2 * SPOTS]
    f_ref, panel, wide, gap_row, sems, wide_sem, gap_sem, *buffers = refs[2 * SPOTS :]
    core, x, z = place_of(here_ref[0])

    def copies(span):
        for spot in range(*SPANS[span]):
            column = pl.multiple_of(group_of(core, x, z, spot // SPOTS, spot % SPOTS) * GROUP, LANES)
            source = b_ref.at[:, pl.ds(column, GROUP)]
            place = (spot - SPANS[span][0]) * GROUP
            yield pltpu.make_async_copy(source, buffers[span].at[:, pl.ds(place, GROUP)], sems.at[spot])

    gap_copy = pltpu.make_async_copy(gap_ref, gap_row, gap_sem)
    gap_copy.start()
    first = pltpu.make_async_copy(b_ref.at[:, :PANEL], wide, wide_sem)
    first.start()
    for span in range(AHEAD):
        for copy in copies(span):
            copy.start()

    gap_copy.wait()
    gap = gap_row[...]
    moment = 0.15 * jnp.exp(jnp.full(gap.shape, laplace_ref[0], jnp.int32).astype(F32) * np.log(np.float32(1.5)))
    position = lax.broadcasted_iota(jnp.int32, gap.shape, 1)
    factor = jnp.where(position < live_ref[0, 0], jnp.exp(-(gap * moment) * 0.5), 0.0)
    f_ref[...] = jnp.broadcast_to(factor, (LANES, gap.shape[1])).T

    first.wait()
    for half, owner in enumerate((1 - core, core)):
        for c in range(0, HALF, LANES):
            piece = wide[:, pl.ds(pl.multiple_of(owner * HALF + c, LANES), LANES)].astype(F32)
            square = f_ref[...] * f_ref[...]
            panel[:, half * HALF + c : half * HALF + c + LANES] = (piece * square).astype(BF16)

    for span, (start, end) in enumerate(SPANS):
        for copy in copies(span):
            copy.wait()
        if span + AHEAD < len(SPANS):
            for copy in copies(span + AHEAD):
                copy.start()
        product = lax.dot_general(
            buffers[span][...], panel[...], (((0,), (0,)), ((), ())), preferred_element_type=F32
        ).astype(BF16)
        for spot in range(start, end):
            k, m = spot // SPOTS, spot % SPOTS
            rows = slice((spot - start) * GROUP, (spot - start + 1) * GROUP)
            theirs[m][k] = product[rows, :HALF]
            mine[k][m] = product[rows, HALF:]


def gram_parts(here, live, laplace, gap, bvals):
    rows = bvals.shape[0]
    part = jax.ShapeDtypeStruct((SPOTS, GROUP, HALF), BF16)
    return pl.pallas_call(
        gram_body,
        in_specs=[TABLE, TABLE, TABLE, FAR, FAR],
        out_specs=[WHOLE] * (2 * SPOTS + 1),
        out_shape=[part] * (2 * SPOTS) + [jax.ShapeDtypeStruct((rows, LANES), F32)],
        scratch_shapes=[
            pltpu.VMEM((rows, PANEL), BF16),
            pltpu.VMEM((rows, PANEL), BF16),
            pltpu.VMEM((1, rows), F32),
            pltpu.SemaphoreType.DMA((SPOTS * SPOTS,)),
            pltpu.SemaphoreType.DMA,
            pltpu.SemaphoreType.DMA,
        ]
        + [pltpu.VMEM((rows, (end - start) * GROUP), BF16) for start, end in SPANS],
        compiler_params=LARGE,
    )(here, live, laplace, gap, bvals)


BLOCKS = ((0, 128), (128, 384), (384, 768), (768, 1280), (1280, 1536))
HALVES = ((0, 1024), (1024, 1536))


def early_body(here_ref, b_ref, other_ref, own_ref, out_ref, zero_ref, held, result, sems, out_sems):
    zero_ref[...] = jnp.zeros_like(zero_ref)

    def copy(block):
        start, end = BLOCKS[block]
        part = pl.ds(start, end - start)
        return pltpu.make_async_copy(b_ref.at[part], held.at[part], sems.at[block])

    def copy_out(block):
        start, end = BLOCKS[block]
        part = pl.ds(start, end - start)
        return pltpu.make_async_copy(result.at[part], out_ref.at[part], out_sems.at[block])

    for block in range(2):
        copy(block).start()
    core, x, z = place_of(here_ref[0])
    for block, (start, end) in enumerate(BLOCKS):
        copy(block).wait()
        if block + 2 < len(BLOCKS):
            copy(block + 2).start()
        for whose, (owner, part) in enumerate(((1 - core, other_ref), (core, own_ref))):
            left = columns_of(held, start, end, owner, x, z, 0)
            product = jnp.dot(left, part[...].reshape(SPOTS * GROUP, HALF), preferred_element_type=F32)
            result[start:end, whose * HALF : (whose + 1) * HALF] = product
        copy_out(block).start()
    for block in range(len(BLOCKS)):
        copy_out(block).wait()


def columns_of(held, start, end, owner, x, z, k):
    columns = []
    for m in range(SPOTS):
        column = pl.multiple_of(group_of(owner, x, z, k, m) * GROUP, GROUP)
        columns.append(held[start:end, pl.ds(column, GROUP)])
    return jnp.concatenate(columns, axis=1)


def early_panel(here, bvals, other, own):
    rows, aux = bvals.shape
    blocks = pltpu.SemaphoreType.DMA((len(BLOCKS),))
    return pl.pallas_call(
        early_body,
        in_specs=[TABLE, FAR, WHOLE, WHOLE],
        out_specs=[FAR, WHOLE, WHOLE],
        out_shape=[
            pltpu.HBM((rows, PANEL), F32),
            jax.ShapeDtypeStruct((SPOTS, GROUP, HALF), BF16),
            pltpu.VMEM((rows, aux), BF16),
        ],
        scratch_shapes=[pltpu.VMEM((rows, PANEL), F32), blocks, blocks],
        compiler_params=MODEST,
        cost_estimate=SMALL,
    )(here, bvals, other, own)


MODEST = pltpu.CompilerParams(vmem_limit_bytes=16 << 20)
SMALL = pl.CostEstimate(flops=0, bytes_accessed=0, transcendentals=0)


def late_body(steps, whose, is_last, here_ref, held, before_ref, f_ref, *refs):
    parts, (out_ref, before, result, sems, out_sems) = refs[: len(steps)], refs[-5:]
    if not is_last:
        out_ref, zero_ref = refs[len(steps) : len(steps) + 2]
        zero_ref[...] = jnp.zeros_like(zero_ref)
    core, x, z = place_of(here_ref[0])
    owner = core if whose else 1 - core

    def copy(block):
        start, end = HALVES[block]
        part = pl.ds(start, end - start)
        source = before_ref.at[part, pl.ds(whose * HALF if before_ref.shape[1] == PANEL else 0, HALF)]
        return pltpu.make_async_copy(source, before.at[part], sems.at[block])

    def copy_out(block):
        start, end = HALVES[block]
        part = pl.ds(start, end - start)
        target = out_ref.at[part]
        if is_last:
            target = out_ref.at[part, pl.ds(pl.multiple_of(owner * HALF, HALF), HALF)]
        return pltpu.make_async_copy(result.at[part], target, out_sems.at[block])

    for block in range(len(HALVES)):
        copy(block).start()
    for block, (start, end) in enumerate(HALVES):
        middle = (start + end) // 2
        spans = ((start, middle), (middle, end))
        totals = [None, None]
        for part, k in zip(parts, steps):
            right = part[...].reshape(SPOTS * GROUP, HALF)
            for n, (low, high) in enumerate(spans):
                left = columns_of(held, low, high, owner, x, z, k)
                product = jnp.dot(left, right, preferred_element_type=F32)
                totals[n] = product if totals[n] is None else totals[n] + product
        copy(block).wait()
        for total, (low, high) in zip(totals, spans):
            for c in range(0, HALF, LANES):
                piece = total[:, c : c + LANES] + before[low:high, c : c + LANES]
                result[low:high, c : c + LANES] = (piece * f_ref[low:high]).astype(BF16) if is_last else piece
        copy_out(block).start()
    for block in range(len(HALVES)):
        copy_out(block).wait()


def late_panel(steps, whose, here, held, before, factor, parts, out, is_last=True):
    rows = held.shape[0]
    kind = BF16 if is_last else F32
    blocks = pltpu.SemaphoreType.DMA((len(HALVES),))
    extra = [] if out is None else [out]
    return pl.pallas_call(
        functools.partial(late_body, steps, whose, is_last),
        in_specs=[TABLE, WHOLE, FAR, WHOLE] + [WHOLE] * len(parts) + [FAR] * len(extra),
        out_specs=[FAR] + [WHOLE] * (not is_last),
        out_shape=[jax.ShapeDtypeStruct((rows, PANEL), BF16)]
        if is_last
        else [pltpu.HBM((rows, HALF), F32), jax.ShapeDtypeStruct(parts[0].shape, BF16)],
        scratch_shapes=[pltpu.VMEM((rows, HALF), F32), pltpu.VMEM((rows, HALF), kind), blocks, blocks],
        input_output_aliases={4 + len(parts): 0} if extra else {},
        compiler_params=MODEST,
        cost_estimate=SMALL,
    )(here, held, before, factor, *parts, *extra)


def total_of(arrays):
    total = arrays[0].astype(F32)
    for array in arrays[1:]:
        total = total + array.astype(F32)
    return total


def on_device(bvals, gap, live, laplace):
    bvals = bvals[0]
    total_rows = bvals.shape[0] * lax.axis_size("rows")
    here = lax.axis_index("rows").reshape(1)
    parts = gram_parts(here, live, laplace, gap, bvals)
    theirs, mine, factor = parts[:SPOTS], parts[SPOTS : 2 * SPOTS], parts[-1]

    pairs = {k: total_of([mine[k], to_pair(theirs[k])]) for k in (2, 1, 3, 0)}
    held = total_of([pairs[0]] + [along_first(pairs[k].astype(BF16), k) for k in (2, 1, 3)])
    share = total_of([held[0]] + [along_second(held[k].astype(BF16), k) for k in (1, 3, 2)]).astype(BF16)
    whole = (total_of([across(share, 1), across(share, 0)]) / total_rows).astype(BF16)
    rows = {k: along_second(whole, SPOTS - k) for k in (1, 3, 2)}
    row = jnp.stack([whole] + [rows[k] for k in range(1, SPOTS)])
    own = {k: along_first(row, SPOTS - k) for k in (3, 1, 2)}
    early, zeros, held = early_panel(here, bvals, to_pair(row), row)
    own[3] = own[3] + zeros
    other = {3: to_pair(own[3])}
    middle, zeros = late_panel((3,), 1, here, held, early, factor, [own[3]], None, False)
    for k in (1, 2):
        own[k] = own[k] + (zeros + BF16(0.0) * other[3])
        other[k] = to_pair(own[k])
    (result,) = late_panel((1, 2), 1, here, held, middle, factor, [own[k] for k in (1, 2)], None)
    (result,) = late_panel((3, 1, 2), 0, here, held, early, factor, [other[k] for k in (3, 1, 2)], result)
    return result[None]


def solution(mesh):
    in_specs = (P("grp", "rows", None), P("grp", "rows"), P("grp", "rows"), P())
    out_specs = P("grp", "rows", None)
    return jax.shard_map(
        on_device, mesh=mesh, in_specs=in_specs, out_specs=out_specs, check_vma=False
    )
```
